128 devices in a mesh: chan: 32 (over x_hi, z, y), seg: 4 (over x_lo, core).
Axes of the slice: x: 4 (x_hi: 2, x_lo: 2; x = x_hi * 2 + x_lo), y: 4, z: 4, core: 2. Of those that a mesh axis runs over, the one named last changes fastest.
Arguments:
- spectra: bfloat16 [2, 16, 768, 4096], P(None, 'seg', None, 'chan'), may hold values from -50 to 50
- half_width: int32 [768], replicated, may hold values from 2 to 16
- band: int32 [32], replicated, may hold values from 0 to 2, as said below
Outputs:
- correlations: float32 [4096, 3, 128, 256], P(('chan', 'seg'))
The draws below stay inside these ranges and needn't reach their ends.
Inputs may be any that keep to these rules, and one draw needn't show every extreme that they name: band[0] = 2, band[29] = 2, band[30] >= 1.
All inputs are finite; a program needn't handle non-finite values.
Results may differ from the reference program's by a relative error of at most 0.0046.
Values may be sent and summed in bfloat16 or wider, within the bound.
A program may use at most 192 MiB of HBM per device.

```python
import math
import jax
import jax.numpy as jnp
from jax import lax

CH = 128
NF = 768
FLO = 25
NT = 3000
LAGS = 256
SLOTS = 3
SEGS = 16
CHANNELS = 4096
N_CHAN = 32


def draw_spectra(key, part):
    key = jax.random.fold_in(key, 11)
    keys = jax.random.split(key, 4)
    chan_scale = jnp.exp(jax.random.uniform(keys[0], (CHANNELS,), jnp.float32, math.log(0.1), math.log(3.0)))
    freq_scale = jnp.exp(jax.random.uniform(keys[1], (NF, 1), jnp.float32, math.log(0.5), math.log(2.0)))
    seg_scale = jnp.exp(jax.random.uniform(keys[2], (SEGS, 1, CHANNELS), jnp.float32, math.log(0.5), math.log(2.0)))
    base = jnp.clip(jax.random.normal(keys[3], (2, SEGS, NF, CHANNELS), jnp.float32), -4.0, 4.0)
    return (base * chan_scale * freq_scale * seg_scale).astype(jnp.bfloat16)


def draw_band(key, part):
    key = jax.random.fold_in(key, 23)
    values = jax.random.randint(key, (N_CHAN,), 0, SLOTS, dtype=jnp.int32)
    values = values.at[N_CHAN - 2].set(jnp.maximum(values[N_CHAN - 2], 1))
    values = values.at[N_CHAN - 3].set(SLOTS - 1)
    return values.at[0].set(SLOTS - 1)


def touch_ends(drawn, stream_key, low, high):
    spot = [jax.random.randint(jax.random.fold_in(stream_key, axis), (), 0, length) for axis, length in enumerate(drawn.shape)]
    main_axis = drawn.shape.index(max(drawn.shape))
    beside = spot[:main_axis] + [(spot[main_axis] + 1) % drawn.shape[main_axis]] + spot[main_axis + 1:]
    return drawn.at[tuple(spot)].set(low).at[tuple(beside)].set(high)


def setup_inputs(seed: int = 0) -> dict:
    key_list = jax.random.split(jax.random.key(seed), 4)
    spectra = draw_spectra(jax.random.fold_in(key_list[3], 71), 0)
    half_width = touch_ends(jax.random.randint(key_list[1], (NF,), 2, 17), jax.random.fold_in(key_list[1], 1), 2, 16).astype(jnp.int32)
    band = draw_band(jax.random.fold_in(key_list[3], 71), 0)
    return dict(spectra=spectra, half_width=half_width, band=band)


floor_value = 0.2

def band_matrix(half_width):
    bins = half_width.shape[0]
    index = jnp.arange(bins, dtype=jnp.int32)
    lower = jnp.maximum(index - half_width, 0)
    upper = jnp.minimum(index + half_width, bins - 1)
    inside = (index[None, :] >= lower[:, None]) & (index[None, :] <= upper[:, None])
    count = (upper - lower + 1).astype(jnp.float32)
    return jnp.where(inside, 1.0, 0.0).astype(jnp.float32) / count[:, None]

def whiten(block, matrix):
    real_part = block[0].astype(jnp.float32)
    imag_part = block[1].astype(jnp.float32)
    amplitude = jnp.sqrt(real_part * real_part + imag_part * imag_part)
    smooth = jnp.einsum('kj,sjc->skc', matrix, amplitude, precision=lax.Precision.HIGHEST)
    denom = jnp.maximum(smooth, floor_value)
    return jnp.stack([real_part / denom, imag_part / denom]).astype(jnp.bfloat16)

def lag_table(bins, lags):
    index = jnp.arange(bins, dtype=jnp.int32)
    shifts = jnp.arange(lags, dtype=jnp.int32) - lags // 2 + 1
    phase = (FLO + index)[:, None] * shifts[None, :] % NT
    angle = 2.0 * math.pi / NT * phase.astype(jnp.float32)
    return jnp.concatenate([jnp.cos(angle), -jnp.sin(angle)], axis=0).astype(jnp.bfloat16)

def cross_lags(rows, partner, table, norm):
    left_re = jnp.concatenate([rows[0], rows[1]], axis=0).astype(jnp.float32)
    left_im = jnp.concatenate([rows[1], -rows[0]], axis=0).astype(jnp.float32)
    right = jnp.concatenate([partner[0], partner[1]], axis=0).astype(jnp.float32)
    cross_re = jnp.einsum('ska,skb->kab', left_re, right, precision=lax.Precision.HIGHEST)
    cross_im = jnp.einsum('ska,skb->kab', left_im, right, precision=lax.Precision.HIGHEST)
    cross = jnp.concatenate([cross_re, cross_im], axis=0).astype(jnp.bfloat16)
    summed = jnp.einsum('kab,kt->abt', cross.astype(jnp.float32), table.astype(jnp.float32), precision=lax.Precision.HIGHEST)
    return summed * norm

def reference(spectra, half_width, band):
    matrix = band_matrix(half_width)
    table = lag_table(NF, LAGS)
    norm = 1.0 / math.sqrt(SEGS * NF)
    blocks = spectra.reshape(2, SEGS, NF, N_CHAN, CH).transpose(3, 0, 1, 2, 4)
    white = lax.map(lambda block: whiten(block, matrix), blocks)
    padded = jnp.concatenate([white, jnp.zeros((SLOTS - 1,) + white.shape[1:], white.dtype)], axis=0)

    def per_block(block_index):
        rows = lax.dynamic_index_in_dim(white, block_index, 0, keepdims=False)
        results = []
        for offset in range(SLOTS):
            partner = lax.dynamic_index_in_dim(padded, block_index + offset, 0, keepdims=False)
            live = (offset <= band[block_index]) & (block_index + offset < N_CHAN)
            value = lax.cond(live, lambda: cross_lags(rows, partner, table, norm), lambda: jnp.zeros((CH, CH, LAGS), jnp.float32))
            results.append(value)
        return jnp.stack(results, axis=1)
    stacked = lax.map(per_block, jnp.arange(N_CHAN, dtype=jnp.int32))
    return stacked.reshape(CHANNELS, SLOTS, CH, LAGS)
```

```python
from functools import partial
import math

import jax
import jax.numpy as jnp
import numpy as np
from jax import lax
from jax.experimental import pallas as pl
from jax.experimental.pallas import tpu as pltpu
from jax.sharding import PartitionSpec as P

FLO = 25
NT = 3000
LAGS = 256
BINS = 768
BLOCKS = 32
CH = 128
ROWS = 32
REACH = 16
FLOOR = 0.2

PIECES = 12
GROUPS = 8
SPAN = 128
STEPS = BINS // SPAN

MESH = pl.DeviceIdType.MESH
f32 = jnp.float32
bf16 = jnp.bfloat16

(OWN_SIB, OWN_X, NEAR, LEG1, OWN2_SIB, NEAR2, NEAR_SIB, NEAR2_SIB, LEG2, FAR_SIB, FAR_X, FAR2_SIB) = range(12)
FLOWS = 12


def lag_table():
    index = np.arange(BINS, dtype=np.int64)
    shifts = np.arange(LAGS, dtype=np.int64) - LAGS // 2 + 1
    phase = ((FLO + index)[:, None] * shifts[None, :]) % NT
    angle = np.float32(2.0 * math.pi / NT) * phase.astype(np.float32)
    angle = angle.astype(np.float64)
    table = np.stack([np.cos(angle), -np.sin(angle)])
    table = table.reshape(2, STEPS, SPAN, LAGS).transpose(1, 3, 0, 2).reshape(STEPS, LAGS, 2 * SPAN)
    return table.astype(np.float32).astype(jnp.bfloat16)


def dot(a, b):
    return lax.dot_general(a, b, (((1,), (0,)), ((), ())), preferred_element_type=f32)


def dot_nt(a, b):
    return lax.dot_general(a, b, (((1,), (1,)), ((), ())), preferred_element_type=f32)


def kernel(
    norm, spec, half, band, table, out,
    white, relay, amp_hi, amp_lo, turned, pick, diag, cross, acc0, acc, ssem, rsem, osem0, osem,
):
    c = lax.axis_index("chan")
    s = lax.axis_index("seg")
    xl = s // 2
    xq = (s + 2) % 4

    def block_at(d):
        t = lax.rem(c + d + 2 * BLOCKS, BLOCKS)
        return t, jnp.where(t // 16 != c // 16, xq, s)

    sib = (c, xl * 2 + 1 - s % 2)
    across = (c, xq)
    near_to = block_at(-1)
    near_from = block_at(1)
    even = c % 2 == 0
    leg_to = block_at(jnp.where(even, 1, -3))
    leg_from = block_at(jnp.where(even, 3, -1))
    nq = near_from[1]
    nq2 = (nq + 2) % 4
    fq = block_at(2)[1]
    fq2 = (fq + 2) % 4
    rq = leg_from[1]

    barrier = pltpu.get_barrier_semaphore()
    for d in (sib, across, near_to, near_from, leg_to, leg_from):
        pl.semaphore_signal(barrier, inc=1, device_id=d, device_id_type=MESH)
    pl.semaphore_wait(barrier, 6)

    def copy(flow, j):
        here, there, to = {
            OWN_SIB: ((0, s), (0, s), sib),
            OWN_X: ((0, s), (0, s), across),
            NEAR: ((0, s), (1, s), near_to),
            LEG1: ((0, s), None, leg_to),
            OWN2_SIB: ((0, xq), (0, xq), sib),
            NEAR2: ((0, xq), (1, xq), near_to),
            NEAR_SIB: ((1, nq), (1, nq), sib),
            NEAR2_SIB: ((1, nq2), (1, nq2), sib),
            LEG2: (None, (2, rq), leg_to),
            FAR_SIB: ((2, fq), (2, fq), sib),
            FAR_X: ((2, fq), (2, fq), across),
            FAR2_SIB: ((2, fq2), (2, fq2), sib),
        }[flow]
        place = lambda at: relay.at[j] if at is None else white.at[at[0], j, :, at[1]]
        return pltpu.make_async_remote_copy(
            src_ref=place(here), dst_ref=place(there), send_sem=ssem.at[flow, j], recv_sem=rsem.at[flow, j],
            device_id=to, device_id_type=MESH,
        )

    amp_hi[pl.ds(0, REACH), :] = jnp.zeros((REACH, 4 * CH), bf16)
    amp_lo[pl.ds(0, REACH), :] = jnp.zeros((REACH, 4 * CH), bf16)
    amp_hi[pl.ds(REACH + BINS, SPAN - REACH), :] = jnp.zeros((SPAN - REACH, 4 * CH), bf16)
    amp_lo[pl.ds(REACH + BINS, SPAN - REACH), :] = jnp.zeros((SPAN - REACH, 4 * CH), bf16)

    def amplitude(m, carry):
        rows = pl.ds(pl.multiple_of(m * SPAN, SPAN), SPAN)
        to = pl.ds(pl.multiple_of(m * SPAN + REACH, REACH), SPAN)
        for seg in range(4):
            re = spec[0, seg, rows, :].astype(f32)
            im = spec[1, seg, rows, :].astype(f32)
            a = jnp.sqrt(re * re + im * im)
            hi = a.astype(bf16)
            amp_hi[to, seg * CH : (seg + 1) * CH] = hi
            amp_lo[to, seg * CH : (seg + 1) * CH] = (a - hi.astype(f32)).astype(bf16)
        return carry

    lax.fori_loop(0, STEPS, amplitude, 0)

    def whiten(m, carry):
        rows = pl.ds(pl.multiple_of(m * SPAN, SPAN), SPAN)
        window = pl.ds(pl.multiple_of(m * SPAN, SPAN), 2 * SPAN)
        width = jnp.broadcast_to(half[pl.ds(m, 1), :].astype(f32), (SPAN, SPAN)).T
        width2 = jnp.concatenate([width, width], axis=1)
        row = lax.broadcasted_iota(jnp.int32, (SPAN, 2 * SPAN), 0)
        col = lax.broadcasted_iota(jnp.int32, (SPAN, 2 * SPAN), 1)
        inside = jnp.abs(col - REACH - row).astype(f32) <= width2
        inside = jnp.where(inside, 1.0, 0.0).astype(bf16)
        bin_at = (lax.broadcasted_iota(jnp.int32, (SPAN, SPAN), 0) + m * SPAN).astype(f32)
        count = jnp.minimum(bin_at + width, BINS - 1.0) - jnp.maximum(bin_at - width, 0.0) + 1.0
        total = dot(inside, amp_hi[window, :]) + dot(inside, amp_lo[window, :])
        for seg in range(4):
            denom = jnp.maximum(total[:, seg * CH : (seg + 1) * CH] / count, FLOOR)
            for part in range(2):
                turned[pl.ds((part * 4 + seg) * SPAN, SPAN), :] = spec[part, seg, rows, :].astype(f32) / denom
        for b in range(SPAN // 16):
            block = [turned[pl.ds(b * 16 + t, 8, stride=SPAN), :] for t in range(16)]
            block = jnp.concatenate(block, axis=0).astype(bf16)
            j = m * 2 + b // 4
            white[0, j, (b % 4) * 2, s] = block[:64]
            white[0, j, (b % 4) * 2 + 1, s] = block[64:]
        for j in (m * 2, m * 2 + 1):
            for flow in (OWN_X, NEAR, LEG1, OWN_SIB):
                copy(flow, j).start()
        return carry

    lax.fori_loop(0, STEPS, whiten, 0)

    row = lax.broadcasted_iota(jnp.int32, (8 * ROWS, CH), 0)
    col = lax.broadcasted_iota(jnp.int32, (8 * ROWS, CH), 1)
    pick[...] = jnp.where(col == s * ROWS + row // 8, 1.0, 0.0).astype(bf16)
    row = lax.broadcasted_iota(jnp.int32, (8 * ROWS, 256), 0)
    col = lax.broadcasted_iota(jnp.int32, (8 * ROWS, 256), 1)
    diag[...] = jnp.where(row % 8 == (col // 8) % 8, 1.0, 0.0)

    def left(j, g):
        x = white[0, j, g].reshape(256, CH)
        y = x.astype(f32).reshape(32, 8, CH)
        y = jnp.concatenate([y[:, 4:], -y[:, :4]], axis=1).reshape(256, CH).astype(bf16)
        keep = diag[...]
        re = (dot_nt(pick[...], x) * keep).astype(bf16)
        im = (dot_nt(pick[...], y) * keep).astype(bf16)
        return jnp.concatenate([re, im], axis=0)

    def crosses(j, g, slots):
        both = []
        for u in (g, g + 1):
            right = [white[d, j, u].reshape(256, CH) for d in slots]
            right = right[0] if len(right) == 1 else jnp.concatenate(right, axis=1)
            both.append(dot(left(j, u), right).reshape(2 * ROWS, 8, right.shape[1]))
        return jnp.concatenate(both, axis=1).astype(bf16)

    def project(j, count, into, first, last, finish):
        def one(p, carry):
            got = dot(table[j // 2], cross[p])
            if not first:
                got = got + into[p]
            if last:
                into[p] = (got * norm).T
                finish(p)
            else:
                into[p] = got
            return carry

        lax.fori_loop(0, count, one, 0)

    def project_at(j, count, into, mask, finish):
        @pl.when(j == 1)
        def _():
            project(j, count, into, True, False, finish)

        @pl.when((j % 2 == 1) & (j > 1) & (j < PIECES - 1))
        def _():
            project(j, count, into, False, False, finish)

        @pl.when(j == PIECES - 1)
        def _():
            project(j, count, into, False, True, finish)

    def out0(p, h):
        return pltpu.make_async_copy(acc0.at[p, pl.ds(h * CH, CH)], out.at[2 * p + h, 0], osem0.at[p, h])

    def finish0(p):
        for h in range(2):
            out0(p, h).start()

    def compute0(j):
        copy(OWN_SIB, j).wait_recv()
        copy(OWN2_SIB, j).wait_recv()

        def pair(i, carry):
            got = crosses(j, 2 * i, (0,)).reshape(2, ROWS // 2, 2, 16, CH)
            at = (j % 2) * 64 + i * 16
            for part in range(2):
                for h in range(2):
                    bins = pl.ds(pl.multiple_of(part * SPAN + at, 16), 16)
                    cross[pl.ds(0, ROWS // 2), bins, h * CH : (h + 1) * CH] = got[part, :, h]
            return carry

        lax.fori_loop(0, GROUPS // 2, pair, 0)
        project_at(j, ROWS // 2, acc0, None, finish0)

    reach = jnp.minimum(band[c], BLOCKS - 1 - c)

    def out12(p, h):
        return pltpu.make_async_copy(acc.at[p, pl.ds(h * CH, CH)], out.at[p, 1 + h], osem.at[p, h])

    def finish12(p):
        for h in range(2):
            rows = pl.ds(h * CH, CH)
            live = jnp.full((CH, LAGS), reach, jnp.int32) >= h + 1
            acc[p, rows] = jnp.where(live, acc[p, rows], 0.0)
            out12(p, h).start()

    def compute12(j):
        for flow in (NEAR_SIB, NEAR2_SIB, FAR_SIB, FAR2_SIB):
            copy(flow, j).wait_recv()

        def pair(i, carry):
            got = crosses(j, 2 * i, (1, 2)).reshape(2, ROWS, 16, 2 * CH)
            at = (j % 2) * 64 + i * 16
            for part in range(2):
                bins = pl.ds(pl.multiple_of(part * SPAN + at, 16), 16)
                cross[:, bins, :] = got[part]
            return carry

        lax.fori_loop(0, GROUPS // 2, pair, 0)
        project_at(j, ROWS, acc, None, finish12)

    def first_half(j, carry):
        copy(OWN_X, j).wait_recv()
        copy(NEAR2, j).start()
        copy(OWN2_SIB, j).start()
        copy(LEG1, j).wait_recv()
        copy(LEG2, j).start()
        copy(NEAR, j).wait_recv()
        copy(NEAR_SIB, j).start()

        @pl.when(j > 0)
        def _():
            compute0(j - 1)

        return carry

    lax.fori_loop(0, PIECES, first_half, 0)
    compute0(PIECES - 1)

    def far_across(j):
        copy(FAR_X, j).wait_recv()
        copy(FAR2_SIB, j).start()

    def second_half(j, carry):
        copy(LEG2, j).wait_recv()
        copy(FAR_X, j).start()
        copy(FAR_SIB, j).start()
        copy(NEAR2, j).wait_recv()
        copy(NEAR2_SIB, j).start()

        @pl.when(j > 0)
        def _():
            far_across(j - 1)

        @pl.when(j > 1)
        def _():
            compute12(j - 2)

        return carry

    lax.fori_loop(0, PIECES, second_half, 0)
    compute12(PIECES - 2)
    far_across(PIECES - 1)
    compute12(PIECES - 1)

    def sent(j, carry):
        for flow in range(FLOWS):
            copy(flow, j).wait_send()
        return carry

    lax.fori_loop(0, PIECES, sent, 0)

    def written(p, carry):
        for h in range(2):
            out12(p, h).wait()
        return carry

    lax.fori_loop(0, ROWS, written, 0)

    def written0(p, carry):
        for h in range(2):
            out0(p, h).wait()
        return carry

    lax.fori_loop(0, ROWS // 2, written0, 0)


def per_device(table, spectra, half_width, band):
    norm = 1.0 / math.sqrt(4 * spectra.shape[1] * BINS)
    vmem = pl.BlockSpec(memory_space=pltpu.VMEM)
    return pl.pallas_call(
        partial(kernel, norm),
        out_shape=jax.ShapeDtypeStruct((ROWS, 3, CH, LAGS), f32),
        in_specs=[vmem, vmem, pl.BlockSpec(memory_space=pltpu.SMEM), vmem],
        out_specs=pl.BlockSpec(memory_space=pl.ANY),
        scratch_shapes=[
            pltpu.VMEM((3, PIECES, GROUPS, 4, 64, CH), bf16),
            pltpu.VMEM((PIECES, GROUPS, 64, CH), bf16),
            pltpu.VMEM((BINS + SPAN, 4 * CH), bf16),
            pltpu.VMEM((BINS + SPAN, 4 * CH), bf16),
            pltpu.VMEM((8 * SPAN, CH), f32),
            pltpu.VMEM((8 * ROWS, CH), bf16),
            pltpu.VMEM((8 * ROWS, 256), f32),
            pltpu.VMEM((ROWS, 2 * SPAN, 2 * CH), bf16),
            pltpu.VMEM((ROWS // 2, LAGS, 2 * CH), f32),
            pltpu.VMEM((ROWS, LAGS, 2 * CH), f32),
            pltpu.SemaphoreType.DMA((FLOWS, PIECES)),
            pltpu.SemaphoreType.DMA((FLOWS, PIECES)),
            pltpu.SemaphoreType.DMA((ROWS // 2, 2)),
            pltpu.SemaphoreType.DMA((ROWS, 2)),
        ],
        compiler_params=pltpu.CompilerParams(collective_id=0, has_side_effects=True, vmem_limit_bytes=60 * 2**20),
        cost_estimate=pl.CostEstimate(flops=2 * 5_500_000_000, bytes_accessed=16_000_000, transcendentals=0),
    )(spectra, half_width.reshape(STEPS, SPAN), band, table)


def solution(mesh):
    table = lag_table()

    def body(spectra, half_width, band):
        return per_device(jnp.asarray(table), spectra, half_width, band)

    in_specs = (P(None, "seg", None, "chan"), P(), P())
    out_specs = P(("chan", "seg"), None, None, None)
    return jax.shard_map(body, mesh=mesh, in_specs=in_specs, out_specs=out_specs, check_vma=False)
```

```python
from functools import partial
import math

import jax
import jax.numpy as jnp
import numpy as np
from jax import lax
from jax.experimental import pallas as pl
from jax.experimental.pallas import tpu as pltpu
from jax.sharding import PartitionSpec as P

FLO = 25
NT = 3000
LAGS = 256
BINS = 768
BLOCKS = 32
CH = 128
ROWS = 32
REACH = 16
FLOOR = 0.2

PIECES = 12
GROUPS = 8
SPAN = 128
STEPS = BINS // SPAN
VMEM_GATHER = 44 * 2**20

MESH = pl.DeviceIdType.MESH
f32 = jnp.float32
bf16 = jnp.bfloat16

(OWN_SIB, OWN_X, NEAR, LEG1, OWN2_SIB, NEAR2, NEAR_SIB, NEAR2_SIB, LEG2, FAR_SIB, FAR_X, FAR2_SIB) = range(12)
FLOWS = 12


def lag_table():
    index = np.arange(BINS, dtype=np.int64)
    shifts = np.arange(LAGS, dtype=np.int64) - LAGS // 2 + 1
    phase = ((FLO + index)[:, None] * shifts[None, :]) % NT
    angle = np.float32(2.0 * math.pi / NT) * phase.astype(np.float32)
    angle = angle.astype(np.float64)
    table = np.stack([np.cos(angle), -np.sin(angle)])
    table = table.reshape(2, STEPS, SPAN, LAGS).transpose(1, 3, 0, 2).reshape(STEPS, LAGS, 2 * SPAN)
    return table.astype(np.float32).astype(jnp.bfloat16)


def dot(a, b):
    return lax.dot_general(a, b, (((1,), (0,)), ((), ())), preferred_element_type=f32)


def dot_nt(a, b):
    return lax.dot_general(a, b, (((1,), (1,)), ((), ())), preferred_element_type=f32)


def gather(
    spec, half, table, acc0, acc,
    white, relay, amp_hi, amp_lo, turned, pick, diag, rows32, cross, ssem, rsem,
):
    c = lax.axis_index("chan")
    s = lax.axis_index("seg")
    xl = s // 2
    xq = (s + 2) % 4

    def block_at(d):
        t = lax.rem(c + d + 2 * BLOCKS, BLOCKS)
        return t, jnp.where(t // 16 != c // 16, xq, s)

    sib = (c, xl * 2 + 1 - s % 2)
    across = (c, xq)
    near_to = block_at(-1)
    near_from = block_at(1)
    even = c % 2 == 0
    leg_to = block_at(jnp.where(even, 1, -3))
    leg_from = block_at(jnp.where(even, 3, -1))
    nq = near_from[1]
    nq2 = (nq + 2) % 4
    fq = block_at(2)[1]
    fq2 = (fq + 2) % 4
    rq = leg_from[1]

    barrier = pltpu.get_barrier_semaphore()
    for d in (sib, across, near_to, near_from, leg_to, leg_from):
        pl.semaphore_signal(barrier, inc=1, device_id=d, device_id_type=MESH)
    pl.semaphore_wait(barrier, 6)

    def copy(flow, j):
        here, there, to = {
            OWN_SIB: ((0, s), (0, s), sib),
            OWN_X: ((0, s), (0, s), across),
            NEAR: ((0, s), (1, s), near_to),
            LEG1: ((0, s), None, leg_to),
            OWN2_SIB: ((0, xq), (0, xq), sib),
            NEAR2: ((0, xq), (1, xq), near_to),
            NEAR_SIB: ((1, nq), (1, nq), sib),
            NEAR2_SIB: ((1, nq2), (1, nq2), sib),
            LEG2: (None, (2, rq), leg_to),
            FAR_SIB: ((2, fq), (2, fq), sib),
            FAR_X: ((2, fq), (2, fq), across),
            FAR2_SIB: ((2, fq2), (2, fq2), sib),
        }[flow]
        place = lambda at: relay.at[j] if at is None else white.at[at[0], j, :, at[1]]
        return pltpu.make_async_remote_copy(
            src_ref=place(here), dst_ref=place(there), send_sem=ssem.at[flow, j], recv_sem=rsem.at[flow, j],
            device_id=to, device_id_type=MESH,
        )

    amp_hi[pl.ds(0, REACH), :] = jnp.zeros((REACH, 4 * CH), bf16)
    amp_lo[pl.ds(0, REACH), :] = jnp.zeros((REACH, 4 * CH), bf16)
    amp_hi[pl.ds(REACH + BINS, SPAN - REACH), :] = jnp.zeros((SPAN - REACH, 4 * CH), bf16)
    amp_lo[pl.ds(REACH + BINS, SPAN - REACH), :] = jnp.zeros((SPAN - REACH, 4 * CH), bf16)

    def amplitude(m, carry):
        rows = pl.ds(pl.multiple_of(m * SPAN, SPAN), SPAN)
        to = pl.ds(pl.multiple_of(m * SPAN + REACH, REACH), SPAN)
        for seg in range(4):
            re = spec[0, seg, rows, :].astype(f32)
            im = spec[1, seg, rows, :].astype(f32)
            a = jnp.sqrt(re * re + im * im)
            hi = a.astype(bf16)
            amp_hi[to, seg * CH : (seg + 1) * CH] = hi
            amp_lo[to, seg * CH : (seg + 1) * CH] = (a - hi.astype(f32)).astype(bf16)
        return carry

    amplitude(0, 0)

    def whiten(m, carry):
        @pl.when(m < STEPS - 1)
        def _():
            amplitude(m + 1, 0)

        rows = pl.ds(pl.multiple_of(m * SPAN, SPAN), SPAN)
        window = pl.ds(pl.multiple_of(m * SPAN, SPAN), 2 * SPAN)
        width = jnp.broadcast_to(half[pl.ds(m, 1), :].astype(f32), (SPAN, SPAN)).T
        width2 = jnp.concatenate([width, width], axis=1)
        row = lax.broadcasted_iota(jnp.int32, (SPAN, 2 * SPAN), 0)
        col = lax.broadcasted_iota(jnp.int32, (SPAN, 2 * SPAN), 1)
        inside = jnp.abs(col - REACH - row).astype(f32) <= width2
        inside = jnp.where(inside, 1.0, 0.0).astype(bf16)
        bin_at = (lax.broadcasted_iota(jnp.int32, (SPAN, SPAN), 0) + m * SPAN).astype(f32)
        count = jnp.minimum(bin_at + width, BINS - 1.0) - jnp.maximum(bin_at - width, 0.0) + 1.0
        total = dot(inside, amp_hi[window, :]) + dot(inside, amp_lo[window, :])
        for seg in range(4):
            denom = jnp.maximum(total[:, seg * CH : (seg + 1) * CH] / count, FLOOR)
            for part in range(2):
                turned[pl.ds((part * 4 + seg) * SPAN, SPAN), :] = spec[part, seg, rows, :].astype(f32) / denom
        for b in range(SPAN // 16):
            block = [turned[pl.ds(b * 16 + t, 8, stride=SPAN), :] for t in range(16)]
            block = jnp.concatenate(block, axis=0).astype(bf16)
            j = m * 2 + b // 4
            white[0, j, (b % 4) * 2, s] = block[:64]
            white[0, j, (b % 4) * 2 + 1, s] = block[64:]
        for j in (m * 2, m * 2 + 1):
            for flow in (OWN_X, NEAR, LEG1, OWN_SIB):
                copy(flow, j).start()
        return carry

    lax.fori_loop(0, STEPS, whiten, 0)

    row = lax.broadcasted_iota(jnp.int32, (ROWS, CH), 0)
    col = lax.broadcasted_iota(jnp.int32, (ROWS, CH), 1)
    pick[...] = jnp.where(col == s * ROWS + row, 1.0, 0.0).astype(bf16)
    row = lax.broadcasted_iota(jnp.int32, (8, 256), 0)
    col = lax.broadcasted_iota(jnp.int32, (8, 256), 1)
    diag[...] = jnp.where(row == (col // 8) % 8, 1.0, 0.0)

    def turn_rows(j, g):
        re = dot_nt(pick[...], white[0, j, g].reshape(256, CH))
        col = lax.broadcasted_iota(jnp.int32, (ROWS, 256), 1)
        rows32[j * GROUPS + g, :ROWS] = re
        rows32[j * GROUPS + g, ROWS:] = jnp.where(col % 8 < 4, pltpu.roll(re, 252, 1), -pltpu.roll(re, 4, 1))

    def left(j, g):
        at = j * GROUPS + g
        keep = diag[...]
        parts = [jnp.broadcast_to(rows32[at, pl.ds(r, 1), :], (8, 256)) * keep for r in range(2 * ROWS)]
        return jnp.concatenate(parts, axis=0).astype(bf16)

    def crosses(j, g, slots):
        both = []
        for u in (g, g + 1):
            right = [white[d, j, u].reshape(256, CH) for d in slots]
            right = right[0] if len(right) == 1 else jnp.concatenate(right, axis=1)
            both.append(dot(left(j, u), right).reshape(2 * ROWS, 8, right.shape[1]))
        return jnp.concatenate(both, axis=1).astype(bf16)

    def project(j, count, into, first):
        def some(q, carry):
            for u in range(8):
                p = q * 8 + u
                got = dot(table[j // 2], cross[p])
                into[p] = got if first else into[p] + got
            return carry

        lax.fori_loop(0, count // 8, some, 0)

    def project_at(j, count, into):
        @pl.when(j == 1)
        def _():
            project(j, count, into, True)

        @pl.when((j % 2 == 1) & (j > 1))
        def _():
            project(j, count, into, False)

    def bins_at(j, i, part):
        return pl.ds(pl.multiple_of(part * SPAN + (j % 2) * 64 + i * 16, 16), 16)

    def compute0(j):
        copy(OWN_SIB, j).wait_recv()
        copy(OWN2_SIB, j).wait_recv()
        for g in range(GROUPS):
            turn_rows(j, g)
        for i in range(GROUPS // 2):
            got = crosses(j, 2 * i, (0,)).reshape(2, ROWS // 2, 2, 16, CH)
            for part in range(2):
                for h in range(2):
                    cross[pl.ds(0, ROWS // 2), bins_at(j, i, part), h * CH : (h + 1) * CH] = got[part, :, h]
        project_at(j, ROWS // 2, acc0)

    def compute12(j):
        for flow in (NEAR_SIB, NEAR2_SIB, FAR_SIB, FAR2_SIB):
            copy(flow, j).wait_recv()
        for i in range(GROUPS // 2):
            got = crosses(j, 2 * i, (1, 2)).reshape(2, ROWS, 16, 2 * CH)
            for part in range(2):
                cross[:, bins_at(j, i, part), :] = got[part]
        project_at(j, ROWS, acc)

    def first_half(j, carry):
        copy(OWN_X, j).wait_recv()
        copy(NEAR2, j).start()
        copy(OWN2_SIB, j).start()
        copy(LEG1, j).wait_recv()
        copy(LEG2, j).start()
        copy(NEAR, j).wait_recv()
        copy(NEAR_SIB, j).start()

        @pl.when(j > 0)
        def _():
            compute0(j - 1)

        return carry

    lax.fori_loop(0, PIECES, first_half, 0)
    compute0(PIECES - 1)

    def far_across(j):
        copy(FAR_X, j).wait_recv()
        copy(FAR2_SIB, j).start()

    def second_half(j, carry):
        copy(LEG2, j).wait_recv()
        copy(FAR_X, j).start()
        copy(FAR_SIB, j).start()
        copy(NEAR2, j).wait_recv()
        copy(NEAR2_SIB, j).start()

        @pl.when(j > 0)
        def _():
            far_across(j - 1)

        @pl.when(j > 1)
        def _():
            compute12(j - 2)

        return carry

    lax.fori_loop(0, PIECES, second_half, 0)
    compute12(PIECES - 2)
    far_across(PIECES - 1)
    compute12(PIECES - 1)

    def sent(j, carry):
        for flow in range(FLOWS):
            copy(flow, j).wait_send()
        return carry

    lax.fori_loop(0, PIECES, sent, 0)


def finish(norm, band, acc0, acc, out):
    c = lax.axis_index("chan")
    reach = jnp.minimum(band[c], BLOCKS - 1 - c)
    p = pl.program_id(0)
    for h in range(2):
        out[h, 0] = (acc0[p, :, h * CH : (h + 1) * CH] * norm).T
        for d in (1, 2):
            live = jnp.full((CH, LAGS), reach, jnp.int32) >= d
            out[h, d] = jnp.where(live, (acc[2 * p + h, :, (d - 1) * CH : d * CH] * norm).T, 0.0)


def per_device(table, spectra, half_width, band):
    norm = 1.0 / math.sqrt(4 * spectra.shape[1] * BINS)
    vmem = pl.BlockSpec(memory_space=pltpu.VMEM)
    smem = pl.BlockSpec(memory_space=pltpu.SMEM)
    acc0, acc = pl.pallas_call(
        gather,
        out_shape=[pltpu.VMEM((ROWS // 2, LAGS, 2 * CH), f32), pltpu.VMEM((ROWS, LAGS, 2 * CH), f32)],
        in_specs=[vmem, vmem, vmem],
        out_specs=[vmem, vmem],
        scratch_shapes=[
            pltpu.VMEM((3, PIECES, GROUPS, 4, 64, CH), bf16),
            pltpu.VMEM((PIECES, GROUPS, 64, CH), bf16),
            pltpu.VMEM((BINS + SPAN, 4 * CH), bf16),
            pltpu.VMEM((BINS + SPAN, 4 * CH), bf16),
            pltpu.VMEM((8 * SPAN, CH), f32),
            pltpu.VMEM((ROWS, CH), bf16),
            pltpu.VMEM((8, 256), f32),
            pltpu.VMEM((PIECES * GROUPS, 2 * ROWS, 256), f32),
            pltpu.VMEM((ROWS, 2 * SPAN, 2 * CH), bf16),
            pltpu.SemaphoreType.DMA((FLOWS, PIECES)),
            pltpu.SemaphoreType.DMA((FLOWS, PIECES)),
        ],
        compiler_params=pltpu.CompilerParams(collective_id=0, has_side_effects=True, vmem_limit_bytes=VMEM_GATHER),
        cost_estimate=pl.CostEstimate(flops=2 * 5_500_000_000, bytes_accessed=16_000_000, transcendentals=0),
        name="gather",
    )(spectra, half_width.reshape(STEPS, SPAN), table)
    acc0 = pltpu.with_memory_space_constraint(acc0, pltpu.VMEM)
    acc = pltpu.with_memory_space_constraint(acc, pltpu.VMEM)
    return pl.pallas_call(
        partial(finish, norm),
        grid=(ROWS // 2,),
        out_shape=jax.ShapeDtypeStruct((ROWS, 3, CH, LAGS), f32),
        in_specs=[smem, vmem, vmem],
        out_specs=pl.BlockSpec((2, 3, CH, LAGS), lambda p: (p, 0, 0, 0)),
        compiler_params=pltpu.CompilerParams(vmem_limit_bytes=8 * 2**20),
        cost_estimate=pl.CostEstimate(flops=0, bytes_accessed=12_600_000, transcendentals=0),
        name="finish",
    )(band, acc0, acc)


def solution(mesh):
    table = lag_table()

    def body(spectra, half_width, band):
        return per_device(jnp.asarray(table), spectra, half_width, band)

    in_specs = (P(None, "seg", None, "chan"), P(), P())
    out_specs = P(("chan", "seg"), None, None, None)
    return jax.shard_map(body, mesh=mesh, in_specs=in_specs, out_specs=out_specs, check_vma=False)
```

```python
from functools import partial
import math

import jax
import jax.numpy as jnp
import numpy as np
from jax import lax
from jax.experimental import pallas as pl
from jax.experimental.pallas import tpu as pltpu
from jax.sharding import PartitionSpec as P

FLO = 25
NT = 3000
LAGS = 256
BINS = 768
BLOCKS = 32
CH = 128
ROWS = 32
REACH = 16
FLOOR = 0.2

PIECES = 12
WINDOW = 3
LAG_FAR, LAG_ACROSS, LAG_LAST = 2, 4, 5
GROUPS = BINS // 8 // PIECES
SPAN = 128
STEPS = BINS // SPAN
SHARE = PIECES // STEPS
VMEM_GATHER = 40 * 2**20
VMEM_FINISH = 20 * 2**20

MESH = pl.DeviceIdType.MESH
f32 = jnp.float32
bf16 = jnp.bfloat16

(OWN_SIB, OWN_X, NEAR, LEG1, OWN2_SIB, NEAR2, NEAR_SIB, NEAR2_SIB, LEG2, FAR_SIB, FAR_X, FAR2_SIB) = range(12)
FLOWS = 12


def lag_table():
    index = np.arange(BINS, dtype=np.int64)
    shifts = np.arange(LAGS, dtype=np.int64) - LAGS // 2 + 1
    phase = ((FLO + index)[:, None] * shifts[None, :]) % NT
    angle = np.float32(2.0 * math.pi / NT) * phase.astype(np.float32)
    angle = angle.astype(np.float64)
    table = np.stack([np.cos(angle), -np.sin(angle)])
    table = table.reshape(2, STEPS, SPAN, LAGS).transpose(1, 3, 0, 2).reshape(STEPS, LAGS, 2 * SPAN)
    return table.astype(np.float32).astype(jnp.bfloat16)


def dot(a, b):
    return lax.dot_general(a, b, (((1,), (0,)), ((), ())), preferred_element_type=f32)


def dot_nt(a, b):
    return lax.dot_general(a, b, (((1,), (1,)), ((), ())), preferred_element_type=f32)


def gather(
    spec, half, table, acc0, acc, cross,
    white, relay, amp_hi, amp_lo, turned, pick, diag, rows32, cross0, ssem, rsem,
):
    c = lax.axis_index("chan")
    s = lax.axis_index("seg")
    xl = s // 2
    xq = (s + 2) % 4

    def block_at(d):
        t = lax.rem(c + d + 2 * BLOCKS, BLOCKS)
        return t, jnp.where(t // 16 != c // 16, xq, s)

    sib = (c, xl * 2 + 1 - s % 2)
    across = (c, xq)
    near_to = block_at(-1)
    near_from = block_at(1)
    even = c % 2 == 0
    leg_to = block_at(jnp.where(even, 1, -3))
    leg_from = block_at(jnp.where(even, 3, -1))
    nq = near_from[1]
    nq2 = (nq + 2) % 4
    fq = block_at(2)[1]
    fq2 = (fq + 2) % 4
    rq = leg_from[1]

    sends_near, gets_near = c > 0, c < BLOCKS - 1
    sends_far, gets_far = c > 1, c < BLOCKS - 2
    relays = leg_from[0] > 1

    barrier = pltpu.get_barrier_semaphore()
    greets = ((sib, None), (across, None), (near_to, sends_near), (near_from, gets_near), (leg_to, c != 1), (leg_from, c != BLOCKS - 2))
    greeted = 0
    for d, present in greets:
        greet = partial(pl.semaphore_signal, barrier, inc=1, device_id=d, device_id_type=MESH)
        if present is None:
            greet()
            greeted = greeted + 1
        else:
            pl.when(present)(greet)
            greeted = greeted + present.astype(jnp.int32)

    def copy(flow, j):
        here, there, to = {
            OWN_SIB: ((0, s), (0, s), sib),
            OWN_X: ((0, s), (0, s), across),
            NEAR: ((0, s), (1, s), near_to),
            LEG1: ((0, s), None, leg_to),
            OWN2_SIB: ((0, xq), (0, xq), sib),
            NEAR2: ((0, xq), (1, xq), near_to),
            NEAR_SIB: ((1, nq), (1, nq), sib),
            NEAR2_SIB: ((1, nq2), (1, nq2), sib),
            LEG2: (None, (2, rq), leg_to),
            FAR_SIB: ((2, fq), (2, fq), sib),
            FAR_X: ((2, fq), (2, fq), across),
            FAR2_SIB: ((2, fq2), (2, fq2), sib),
        }[flow]
        place = lambda at: relay.at[j] if at is None else white.at[at[0], j, at[1]]
        return pltpu.make_async_remote_copy(
            src_ref=place(here), dst_ref=place(there), send_sem=ssem.at[flow, j], recv_sem=rsem.at[flow, j],
            device_id=to, device_id_type=MESH,
        )

    amp_hi[pl.ds(0, REACH), :] = jnp.zeros((REACH, 4 * CH), bf16)
    amp_lo[pl.ds(0, REACH), :] = jnp.zeros((REACH, 4 * CH), bf16)
    amp_hi[pl.ds(REACH + BINS, SPAN - REACH), :] = jnp.zeros((SPAN - REACH, 4 * CH), bf16)
    amp_lo[pl.ds(REACH + BINS, SPAN - REACH), :] = jnp.zeros((SPAN - REACH, 4 * CH), bf16)

    def amplitude(m, carry):
        rows = pl.ds(pl.multiple_of(m * SPAN, SPAN), SPAN)
        to = pl.ds(pl.multiple_of(m * SPAN + REACH, REACH), SPAN)
        for seg in range(4):
            re = spec[0, seg, rows, :].astype(f32)
            im = spec[1, seg, rows, :].astype(f32)
            a = jnp.sqrt(re * re + im * im)
            hi = a.astype(bf16)
            amp_hi[to, seg * CH : (seg + 1) * CH] = hi
            amp_lo[to, seg * CH : (seg + 1) * CH] = (a - hi.astype(f32)).astype(bf16)
        return carry

    def whiten(m, carry):
        @pl.when(m < STEPS - 1)
        def _():
            amplitude(m + 1, 0)

        rows = pl.ds(pl.multiple_of(m * SPAN, SPAN), SPAN)
        window = pl.ds(pl.multiple_of(m * SPAN, SPAN), 2 * SPAN)
        width = jnp.broadcast_to(half[pl.ds(m, 1), :].astype(f32), (SPAN, SPAN)).T
        width2 = jnp.concatenate([width, width], axis=1)
        row = lax.broadcasted_iota(jnp.int32, (SPAN, 2 * SPAN), 0)
        col = lax.broadcasted_iota(jnp.int32, (SPAN, 2 * SPAN), 1)
        inside = jnp.abs(col - REACH - row).astype(f32) <= width2
        inside = jnp.where(inside, 1.0, 0.0).astype(bf16)
        bin_at = (lax.broadcasted_iota(jnp.int32, (SPAN, SPAN), 0) + m * SPAN).astype(f32)
        count = jnp.minimum(bin_at + width, BINS - 1.0) - jnp.maximum(bin_at - width, 0.0) + 1.0
        total = dot(inside, amp_hi[window, :]) + dot(inside, amp_lo[window, :])
        for seg in range(4):
            denom = jnp.maximum(total[:, seg * CH : (seg + 1) * CH] / count, FLOOR)
            for part in range(2):
                turned[pl.ds((part * 4 + seg) * SPAN, SPAN), :] = spec[part, seg, rows, :].astype(f32) / denom
        for b in range(SPAN // 16):
            block = [turned[pl.ds(b * 16 + t, 8, stride=SPAN), :] for t in range(16)]
            block = jnp.concatenate(block, axis=0).astype(bf16)
            j = m * SHARE + (2 * b) // GROUPS
            white[0, j, s, (2 * b) % GROUPS] = block[:64]
            white[0, j, s, (2 * b + 1) % GROUPS] = block[64:]
        return carry

    def send_own(j):
        copy(OWN_X, j).start()
        pl.when(sends_near)(lambda: copy(NEAR, j).start())
        pl.when(sends_far)(lambda: copy(LEG1, j).start())

    amplitude(0, 0)
    whiten(0, 0)
    pl.semaphore_wait(barrier, greeted)
    for j in range(min(WINDOW, SHARE)):
        send_own(j)
    lax.fori_loop(1, STEPS, whiten, 0)
    for j in range(SHARE, WINDOW):
        send_own(j)

    def to_sibling(j, carry):
        copy(OWN_SIB, j).start()
        return carry

    lax.fori_loop(0, PIECES, to_sibling, 0)

    def clear(d):
        def one(j, carry):
            white[d, j] = jnp.zeros(white.shape[2:], bf16)
            return carry

        lax.fori_loop(0, PIECES, one, 0)

    pl.when(jnp.logical_not(gets_near))(lambda: clear(1))
    pl.when(jnp.logical_not(gets_far))(lambda: clear(2))

    row = lax.broadcasted_iota(jnp.int32, (ROWS, CH), 0)
    col = lax.broadcasted_iota(jnp.int32, (ROWS, CH), 1)
    pick[...] = jnp.where(col == s * ROWS + row, 1.0, 0.0).astype(bf16)
    row = lax.broadcasted_iota(jnp.int32, (8, 256), 0)
    col = lax.broadcasted_iota(jnp.int32, (8, 256), 1)
    diag[...] = jnp.where(row == (col // 8) % 8, 1.0, 0.0)

    def group(d, j, g):
        return white[d, j, :, g].reshape(256, CH)

    def turn_rows(j, g):
        re = dot_nt(pick[...], group(0, j, g))
        col = lax.broadcasted_iota(jnp.int32, (ROWS, 256), 1)
        rows32[j * GROUPS + g, :ROWS] = re
        rows32[j * GROUPS + g, ROWS:] = jnp.where(col % 8 < 4, pltpu.roll(re, 252, 1), -pltpu.roll(re, 4, 1))

    def left(j, g):
        at = j * GROUPS + g
        keep = diag[...]
        parts = [jnp.broadcast_to(rows32[at, pl.ds(r, 1), :], (8, 256)) * keep for r in range(2 * ROWS)]
        return jnp.concatenate(parts, axis=0).astype(bf16)

    def crosses(j, g, slots):
        both = []
        for u in (g, g + 1):
            right = [group(d, j, u) for d in slots]
            right = right[0] if len(right) == 1 else jnp.concatenate(right, axis=1)
            both.append(dot(left(j, u), right).reshape(2 * ROWS, 8, right.shape[1]))
        return jnp.concatenate(both, axis=1).astype(bf16)

    def project(j, count, source, into, first):
        def some(q, carry):
            for u in range(8):
                p = q * 8 + u
                got = dot(table[j // SHARE], source[p])
                into[p] = got if first else into[p] + got
            return carry

        lax.fori_loop(0, count // 8, some, 0)

    def project_at(j, count, source, into, pieces):
        pl.when(j == SHARE - 1)(lambda: project(j, count, source, into, True))
        later = (j % SHARE == SHARE - 1) & (j > SHARE - 1) & (j < pieces)
        pl.when(later)(lambda: project(j, count, source, into, False))

    def bins_at(j, i, part):
        return pl.ds(pl.multiple_of(part * SPAN + (j % SHARE) * (8 * GROUPS) + i * 16, 16), 16)

    def compute0(j):
        copy(OWN_SIB, j).wait_recv()
        copy(OWN2_SIB, j).wait_recv()
        for g in range(GROUPS):
            turn_rows(j, g)
        for i in range(GROUPS // 2):
            got = crosses(j, 2 * i, (0,)).reshape(2, ROWS // 2, 2, 16, CH)
            for part in range(2):
                for h in range(2):
                    cross0[:, bins_at(j, i, part), h * CH : (h + 1) * CH] = got[part, :, h]
        project_at(j, ROWS // 2, cross0, acc0, PIECES)

    def compute12(j):
        @pl.when(gets_near)
        def _():
            copy(NEAR_SIB, j).wait_recv()
            copy(NEAR2_SIB, j).wait_recv()

        @pl.when(gets_far)
        def _():
            copy(FAR_SIB, j).wait_recv()
            copy(FAR2_SIB, j).wait_recv()

        for i in range(GROUPS // 2):
            got = crosses(j, 2 * i, (1, 2)).reshape(2, ROWS, 16, 2 * CH)
            for part in range(2):
                cross[:, bins_at(j, i, part), :] = got[part]
        project_at(j, ROWS, cross, acc, PIECES - SHARE)

    def own_arrived(j):
        copy(OWN_X, j).wait_recv()
        pl.when(sends_near)(lambda: copy(NEAR2, j).start())
        copy(OWN2_SIB, j).start()

        @pl.when(relays)
        def _():
            copy(LEG1, j).wait_recv()
            copy(LEG2, j).start()

        @pl.when(gets_near)
        def _():
            copy(NEAR, j).wait_recv()
            copy(NEAR_SIB, j).start()

    def far_arrived(j):
        @pl.when(gets_far)
        def _():
            copy(LEG2, j).wait_recv()
            copy(FAR_X, j).start()
            copy(FAR_SIB, j).start()

        @pl.when(gets_near)
        def _():
            copy(NEAR2, j).wait_recv()
            copy(NEAR2_SIB, j).start()

    def far_across(j):
        @pl.when(gets_far)
        def _():
            copy(FAR_X, j).wait_recv()
            copy(FAR2_SIB, j).start()

    def step(t, carry):
        pl.when(t + WINDOW < PIECES)(lambda: send_own(t + WINDOW))
        pl.when(t < PIECES)(lambda: own_arrived(t))
        pl.when((t >= 1) & (t < PIECES + 1))(lambda: compute0(t - 1))
        pl.when((t >= LAG_FAR) & (t < PIECES + LAG_FAR))(lambda: far_arrived(t - LAG_FAR))
        pl.when((t >= LAG_ACROSS) & (t < PIECES + LAG_ACROSS))(lambda: far_across(t - LAG_ACROSS))
        pl.when(t >= LAG_LAST)(lambda: compute12(t - LAG_LAST))
        return carry

    lax.fori_loop(0, PIECES + LAG_LAST, step, 0)

    def sent(j, carry):
        for flow in (OWN_SIB, OWN_X, OWN2_SIB):
            copy(flow, j).wait_send()
        for flow, present in (
            (NEAR, sends_near), (NEAR2, sends_near), (LEG1, sends_far), (LEG2, relays),
            (NEAR_SIB, gets_near),
            (NEAR2_SIB, gets_near), (FAR_SIB, gets_far), (FAR_X, gets_far), (FAR2_SIB, gets_far),
        ):
            pl.when(present)(copy(flow, j).wait_send)
        return carry

    lax.fori_loop(0, PIECES, sent, 0)


def finish(norm, band, table, acc0, acc, cross, out, stage, sem):
    c = lax.axis_index("chan")
    reach = jnp.minimum(band[c], BLOCKS - 1 - c)

    def write(p):
        return pltpu.make_async_copy(stage.at[pl.ds(2 * p, 2)], out.at[pl.ds(2 * p, 2)], sem.at[p])

    def some(q, carry):
        for p in [4 * q + u for u in range(4)]:
            for h in range(2):
                stage[2 * p + h, 0] = (acc0[p, :, h * CH : (h + 1) * CH] * norm).T
                got = (acc[2 * p + h] + dot(table[...], cross[2 * p + h])) * norm
                for d in (1, 2):
                    live = jnp.full((CH, LAGS), reach, jnp.int32) >= d
                    stage[2 * p + h, d] = jnp.where(live, got[:, (d - 1) * CH : d * CH].T, 0.0)
            write(p).start()
        return carry

    lax.fori_loop(0, ROWS // 8, some, 0)

    def written(p, carry):
        write(p).wait()
        return carry

    lax.fori_loop(0, ROWS // 2, written, 0)


def per_device(table, last, spectra, half_width, band):
    norm = 1.0 / math.sqrt(4 * spectra.shape[1] * BINS)
    vmem = pl.BlockSpec(memory_space=pltpu.VMEM)
    smem = pl.BlockSpec(memory_space=pltpu.SMEM)
    sums = pl.pallas_call(
        gather,
        out_shape=[
            pltpu.VMEM((ROWS // 2, LAGS, 2 * CH), f32),
            pltpu.VMEM((ROWS, LAGS, 2 * CH), f32),
            pltpu.VMEM((ROWS, 2 * SPAN, 2 * CH), bf16),
        ],
        in_specs=[vmem, vmem, vmem],
        out_specs=[vmem, vmem, vmem],
        scratch_shapes=[
            pltpu.VMEM((3, PIECES, 4, GROUPS, 64, CH), bf16),
            pltpu.VMEM((PIECES, GROUPS, 64, CH), bf16),
            pltpu.VMEM((BINS + SPAN, 4 * CH), bf16),
            pltpu.VMEM((BINS + SPAN, 4 * CH), bf16),
            pltpu.VMEM((8 * SPAN, CH), f32),
            pltpu.VMEM((ROWS, CH), bf16),
            pltpu.VMEM((8, 256), f32),
            pltpu.VMEM((PIECES * GROUPS, 2 * ROWS, 256), f32),
            pltpu.VMEM((ROWS // 2, 2 * SPAN, 2 * CH), bf16),
            pltpu.SemaphoreType.DMA((FLOWS, PIECES)),
            pltpu.SemaphoreType.DMA((FLOWS, PIECES)),
        ],
        compiler_params=pltpu.CompilerParams(collective_id=0, has_side_effects=True, vmem_limit_bytes=VMEM_GATHER),
        cost_estimate=pl.CostEstimate(flops=2 * 5_500_000_000, bytes_accessed=16_000_000, transcendentals=0),
        name="gather",
    )(spectra, half_width.reshape(STEPS, SPAN), table)
    sums = [pltpu.with_memory_space_constraint(x, pltpu.VMEM) for x in sums]
    return pl.pallas_call(
        partial(finish, norm),
        out_shape=jax.ShapeDtypeStruct((ROWS, 3, CH, LAGS), f32),
        in_specs=[smem, vmem, vmem, vmem, vmem],
        out_specs=pl.BlockSpec(memory_space=pl.ANY),
        scratch_shapes=[pltpu.VMEM((ROWS, 3, CH, LAGS), f32), pltpu.SemaphoreType.DMA((ROWS // 2,))],
        compiler_params=pltpu.CompilerParams(vmem_limit_bytes=VMEM_FINISH),
        cost_estimate=pl.CostEstimate(flops=2 * 540_000_000, bytes_accessed=12_600_000, transcendentals=0),
        name="finish",
    )(band, last, *sums)


def solution(mesh):
    table = lag_table()

    def body(spectra, half_width, band):
        return per_device(jnp.asarray(table), jnp.asarray(table[-1]), spectra, half_width, band)

    in_specs = (P(None, "seg", None, "chan"), P(), P())
    out_specs = P(("chan", "seg"), None, None, None)
    return jax.shard_map(body, mesh=mesh, in_specs=in_specs, out_specs=out_specs, check_vma=False)
```

```python
from functools import partial
import math

import jax
import jax.numpy as jnp
import numpy as np
from jax import lax
from jax.experimental import pallas as pl
from jax.experimental.pallas import tpu as pltpu
from jax.sharding import PartitionSpec as P

FLO = 25
NT = 3000
LAGS = 256
BINS = 768
BLOCKS = 32
CH = 128
ROWS = 32
REACH = 16
FLOOR = 0.2

PIECES = 12
WINDOW = 3
LAG_FAR, LAG_ACROSS, LAG_LAST = 2, 4, 5
DOWN = (4,)
GROUPS = BINS // 8 // PIECES
SPAN = 128
STEPS = BINS // SPAN
SHARE = PIECES // STEPS
VMEM_GATHER = 40 * 2**20
VMEM_FINISH = 20 * 2**20

MESH = pl.DeviceIdType.MESH
f32 = jnp.float32
bf16 = jnp.bfloat16

(OWN_SIB, OWN_X, NEAR, LEG1, OWN2_SIB, NEAR2, NEAR_SIB, NEAR2_SIB, LEG2, FAR_SIB, FAR_X, FAR2_SIB) = range(12)
FLOWS = 12
DOWN2, NEAR_X = range(FLOWS, FLOWS + 2)


def lag_table():
    index = np.arange(BINS, dtype=np.int64)
    shifts = np.arange(LAGS, dtype=np.int64) - LAGS // 2 + 1
    phase = ((FLO + index)[:, None] * shifts[None, :]) % NT
    angle = np.float32(2.0 * math.pi / NT) * phase.astype(np.float32)
    angle = angle.astype(np.float64)
    table = np.stack([np.cos(angle), -np.sin(angle)])
    table = table.reshape(2, STEPS, SPAN, LAGS).transpose(1, 3, 0, 2).reshape(STEPS, LAGS, 2 * SPAN)
    return table.astype(np.float32).astype(jnp.bfloat16)


def dot(a, b):
    return lax.dot_general(a, b, (((1,), (0,)), ((), ())), preferred_element_type=f32)


def dot_nt(a, b):
    return lax.dot_general(a, b, (((1,), (1,)), ((), ())), preferred_element_type=f32)


def gather(
    spec_hbm, half, table_hbm, acc0, acc, cross,
    spec, table, load_sem, white, relay, amp_hi, amp_lo, turned, pick, diag, rows32, cross0, ssem, rsem,
):
    def load(m):
        rows = pl.ds(m * SPAN, SPAN)
        return pltpu.make_async_copy(spec_hbm.at[:, :, rows], spec.at[:, :, rows], load_sem.at[m])

    load_table = pltpu.make_async_copy(table_hbm, table, load_sem.at[STEPS])
    for m in range(STEPS):
        load(m).start()
    load_table.start()

    c = lax.axis_index("chan")
    s = lax.axis_index("seg")
    xl = s // 2
    xq = (s + 2) % 4

    def block_at(d):
        t = lax.rem(c + d + 2 * BLOCKS, BLOCKS)
        return t, jnp.where(t // 16 != c // 16, xq, s)

    sib = (c, xl * 2 + 1 - s % 2)
    across = (c, xq)
    near_to = block_at(-1)
    near_from = block_at(1)
    even = c % 2 == 0
    leg_to = block_at(jnp.where(even, 1, -3))
    leg_from = block_at(jnp.where(even, 3, -1))
    nq = near_from[1]
    nq2 = (nq + 2) % 4
    fq = block_at(2)[1]
    fq2 = (fq + 2) % 4
    rq = leg_from[1]

    sends_near, gets_near = c > 0, c < BLOCKS - 1
    sends_far, gets_far = c > 1, c < BLOCKS - 2
    relays = leg_from[0] > 1
    passes_down = sends_near & gets_near

    barrier = pltpu.get_barrier_semaphore()
    greets = ((sib, None), (across, None), (near_to, sends_near), (near_from, gets_near), (leg_to, c != 1), (leg_from, c != BLOCKS - 2))
    greeted = 0
    for d, present in greets:
        greet = partial(pl.semaphore_signal, barrier, inc=1, device_id=d, device_id_type=MESH)
        if present is None:
            greet()
            greeted = greeted + 1
        else:
            pl.when(present)(greet)
            greeted = greeted + present.astype(jnp.int32)

    def copy(flow, j):
        here, there, to, *slot = {
            OWN_SIB: ((0, s), (0, s), sib),
            OWN_X: ((0, s), (0, s), across),
            NEAR: ((0, s), (1, s), near_to),
            LEG1: ((0, s), None, leg_to),
            OWN2_SIB: ((0, xq), (0, xq), sib),
            NEAR2: ((0, xq), (1, xq), near_to),
            NEAR_SIB: ((1, nq), (1, nq), sib),
            NEAR2_SIB: ((1, nq2), (1, nq2), sib),
            LEG2: (None, (2, rq), leg_to),
            FAR_SIB: ((2, fq), (2, fq), sib),
            FAR_X: ((2, fq), (2, fq), across),
            FAR2_SIB: ((2, fq2), (2, fq2), sib),
            DOWN2: ((1, nq), (2, nq), near_to, LEG2),
            NEAR_X: ((1, nq), (1, nq), across, NEAR2),
        }[flow]
        slot = slot[0] if slot else flow
        place = lambda at: relay.at[j] if at is None else white.at[at[0], j, at[1]]
        return pltpu.make_async_remote_copy(
            src_ref=place(here), dst_ref=place(there), send_sem=ssem.at[slot, j], recv_sem=rsem.at[slot, j],
            device_id=to, device_id_type=MESH,
        )

    def start(present, flow, j):
        pl.when(present)(lambda: copy(flow, j).start())

    def plain(j):
        hit = j != DOWN[0]
        for v in DOWN[1:]:
            hit = hit & (j != v)
        return jnp.asarray(hit)

    def down(j):
        return jnp.logical_not(plain(j))

    amp_hi[pl.ds(0, REACH), :] = jnp.zeros((REACH, 4 * CH), bf16)
    amp_lo[pl.ds(0, REACH), :] = jnp.zeros((REACH, 4 * CH), bf16)
    amp_hi[pl.ds(REACH + BINS, SPAN - REACH), :] = jnp.zeros((SPAN - REACH, 4 * CH), bf16)
    amp_lo[pl.ds(REACH + BINS, SPAN - REACH), :] = jnp.zeros((SPAN - REACH, 4 * CH), bf16)

    def amplitude(m, carry):
        load(m).wait()
        rows = pl.ds(pl.multiple_of(m * SPAN, SPAN), SPAN)
        to = pl.ds(pl.multiple_of(m * SPAN + REACH, REACH), SPAN)
        for seg in range(4):
            re = spec[0, seg, rows, :].astype(f32)
            im = spec[1, seg, rows, :].astype(f32)
            a = jnp.sqrt(re * re + im * im)
            hi = a.astype(bf16)
            amp_hi[to, seg * CH : (seg + 1) * CH] = hi
            amp_lo[to, seg * CH : (seg + 1) * CH] = (a - hi.astype(f32)).astype(bf16)
        return carry

    def whiten(m, carry):
        @pl.when(m < STEPS - 1)
        def _():
            amplitude(m + 1, 0)

        rows = pl.ds(pl.multiple_of(m * SPAN, SPAN), SPAN)
        window = pl.ds(pl.multiple_of(m * SPAN, SPAN), 2 * SPAN)
        width = jnp.broadcast_to(half[pl.ds(m, 1), :].astype(f32), (SPAN, SPAN)).T
        width2 = jnp.concatenate([width, width], axis=1)
        row = lax.broadcasted_iota(jnp.int32, (SPAN, 2 * SPAN), 0)
        col = lax.broadcasted_iota(jnp.int32, (SPAN, 2 * SPAN), 1)
        inside = jnp.abs(col - REACH - row).astype(f32) <= width2
        inside = jnp.where(inside, 1.0, 0.0).astype(bf16)
        bin_at = (lax.broadcasted_iota(jnp.int32, (SPAN, SPAN), 0) + m * SPAN).astype(f32)
        count = jnp.minimum(bin_at + width, BINS - 1.0) - jnp.maximum(bin_at - width, 0.0) + 1.0
        total = dot(inside, amp_hi[window, :]) + dot(inside, amp_lo[window, :])
        for seg in range(4):
            denom = jnp.maximum(total[:, seg * CH : (seg + 1) * CH] / count, FLOOR)
            for part in range(2):
                turned[pl.ds((part * 4 + seg) * SPAN, SPAN), :] = spec[part, seg, rows, :].astype(f32) / denom
        for b in range(SPAN // 16):
            block = [turned[pl.ds(b * 16 + t, 8, stride=SPAN), :] for t in range(16)]
            block = jnp.concatenate(block, axis=0).astype(bf16)
            j = m * SHARE + (2 * b) // GROUPS
            white[0, j, s, (2 * b) % GROUPS] = block[:64]
            white[0, j, s, (2 * b + 1) % GROUPS] = block[64:]
        return carry

    def send_own(j):
        copy(OWN_X, j).start()
        start(sends_near, NEAR, j)
        start(sends_far & plain(j), LEG1, j)

    amplitude(0, 0)
    whiten(0, 0)
    pl.semaphore_wait(barrier, greeted)
    for j in range(min(WINDOW, SHARE)):
        send_own(j)
    lax.fori_loop(1, STEPS, whiten, 0)
    for j in range(SHARE, WINDOW):
        send_own(j)

    def to_sibling(j, carry):
        copy(OWN_SIB, j).start()
        return carry

    lax.fori_loop(0, PIECES, to_sibling, 0)
    load_table.wait()

    def clear(d):
        def one(j, carry):
            white[d, j] = jnp.zeros(white.shape[2:], bf16)
            return carry

        lax.fori_loop(0, PIECES, one, 0)

    pl.when(jnp.logical_not(gets_near))(lambda: clear(1))
    pl.when(jnp.logical_not(gets_far))(lambda: clear(2))

    row = lax.broadcasted_iota(jnp.int32, (ROWS, CH), 0)
    col = lax.broadcasted_iota(jnp.int32, (ROWS, CH), 1)
    pick[...] = jnp.where(col == s * ROWS + row, 1.0, 0.0).astype(bf16)
    row = lax.broadcasted_iota(jnp.int32, (8, 256), 0)
    col = lax.broadcasted_iota(jnp.int32, (8, 256), 1)
    diag[...] = jnp.where(row == (col // 8) % 8, 1.0, 0.0)

    def group(d, j, g):
        return white[d, j, :, g].reshape(256, CH)

    def turn_rows(j, g):
        re = dot_nt(pick[...], group(0, j, g))
        col = lax.broadcasted_iota(jnp.int32, (ROWS, 256), 1)
        rows32[j * GROUPS + g, :ROWS] = re
        rows32[j * GROUPS + g, ROWS:] = jnp.where(col % 8 < 4, pltpu.roll(re, 252, 1), -pltpu.roll(re, 4, 1))

    def left(j, g):
        at = j * GROUPS + g
        keep = diag[...]
        parts = [jnp.broadcast_to(rows32[at, pl.ds(r, 1), :], (8, 256)) * keep for r in range(2 * ROWS)]
        return jnp.concatenate(parts, axis=0).astype(bf16)

    def crosses(j, g, slots):
        both = []
        for u in (g, g + 1):
            right = [group(d, j, u) for d in slots]
            right = right[0] if len(right) == 1 else jnp.concatenate(right, axis=1)
            both.append(dot(left(j, u), right).reshape(2 * ROWS, 8, right.shape[1]))
        return jnp.concatenate(both, axis=1).astype(bf16)

    def project(j, count, source, into, first):
        def some(q, carry):
            for u in range(8):
                p = q * 8 + u
                got = dot(table[j // SHARE], source[p])
                into[p] = got if first else into[p] + got
            return carry

        lax.fori_loop(0, count // 8, some, 0)

    def project_at(j, count, source, into, pieces):
        pl.when(j == SHARE - 1)(lambda: project(j, count, source, into, True))
        later = (j % SHARE == SHARE - 1) & (j > SHARE - 1) & (j < pieces)
        pl.when(later)(lambda: project(j, count, source, into, False))

    def bins_at(j, i, part):
        return pl.ds(pl.multiple_of(part * SPAN + (j % SHARE) * (8 * GROUPS) + i * 16, 16), 16)

    def compute0(j):
        copy(OWN_SIB, j).wait_recv()
        copy(OWN2_SIB, j).wait_recv()
        for g in range(GROUPS):
            turn_rows(j, g)
        for i in range(GROUPS // 2):
            got = crosses(j, 2 * i, (0,)).reshape(2, ROWS // 2, 2, 16, CH)
            for part in range(2):
                for h in range(2):
                    cross0[:, bins_at(j, i, part), h * CH : (h + 1) * CH] = got[part, :, h]
        project_at(j, ROWS // 2, cross0, acc0, PIECES)

    def compute12(j):
        @pl.when(gets_near)
        def _():
            copy(NEAR_SIB, j).wait_recv()
            copy(NEAR2_SIB, j).wait_recv()

        @pl.when(gets_far)
        def _():
            copy(FAR_SIB, j).wait_recv()
            copy(FAR2_SIB, j).wait_recv()

        for i in range(GROUPS // 2):
            got = crosses(j, 2 * i, (1, 2)).reshape(2, ROWS, 16, 2 * CH)
            for part in range(2):
                cross[:, bins_at(j, i, part), :] = got[part]
        project_at(j, ROWS, cross, acc, PIECES - SHARE)

    def own_arrived(j):
        copy(OWN_X, j).wait_recv()
        start(sends_near & plain(j), NEAR2, j)
        copy(OWN2_SIB, j).start()

        @pl.when(relays & plain(j))
        def _():
            copy(LEG1, j).wait_recv()
            copy(LEG2, j).start()

        @pl.when(gets_near)
        def _():
            copy(NEAR, j).wait_recv()
            start(sends_near & down(j), DOWN2, j)
            start(down(j), NEAR_X, j)
            copy(NEAR_SIB, j).start()

    def far_arrived(j):
        @pl.when(gets_far)
        def _():
            copy(LEG2, j).wait_recv()
            copy(FAR_X, j).start()
            copy(FAR_SIB, j).start()

        @pl.when(gets_near)
        def _():
            copy(NEAR2, j).wait_recv()
            copy(NEAR2_SIB, j).start()

    def far_across(j):
        @pl.when(gets_far)
        def _():
            copy(FAR_X, j).wait_recv()
            copy(FAR2_SIB, j).start()

    def sent(j):
        for flow in (OWN_SIB, OWN_X, OWN2_SIB):
            copy(flow, j).wait_send()
        for flow, present in (
            (NEAR, sends_near), (NEAR_SIB, gets_near), (NEAR2_SIB, gets_near), (FAR_SIB, gets_far), (FAR_X, gets_far),
            (FAR2_SIB, gets_far), (LEG1, sends_far & plain(j)), (LEG2, relays & plain(j)), (NEAR2, sends_near & plain(j)),
            (DOWN2, passes_down & down(j)), (NEAR_X, gets_near & down(j)),
        ):
            pl.when(present)(copy(flow, j).wait_send)

    def step(t, carry):
        pl.when(t + WINDOW < PIECES)(lambda: send_own(t + WINDOW))
        pl.when(t < PIECES)(lambda: own_arrived(t))
        pl.when((t >= 1) & (t < PIECES + 1))(lambda: compute0(t - 1))
        pl.when((t >= LAG_FAR) & (t < PIECES + LAG_FAR))(lambda: far_arrived(t - LAG_FAR))
        pl.when((t >= LAG_ACROSS) & (t < PIECES + LAG_ACROSS))(lambda: far_across(t - LAG_ACROSS))
        pl.when(t >= LAG_LAST)(lambda: compute12(t - LAG_LAST))
        pl.when(t >= LAG_LAST)(lambda: sent(t - LAG_LAST))
        return carry

    lax.fori_loop(0, PIECES + LAG_LAST, step, 0)


def finish(norm, band, table, acc0, acc, cross, out, stage, sem):
    c = lax.axis_index("chan")
    reach = jnp.minimum(band[c], BLOCKS - 1 - c)

    def write(a):
        return pltpu.make_async_copy(stage.at[a], out.at[a], sem.at[a])

    def some(q, carry):
        for p in [4 * q + u for u in range(4)]:
            for h in range(2):
                stage[2 * p + h, 0] = (acc0[p, :, h * CH : (h + 1) * CH] * norm).T
                got = (acc[2 * p + h] + dot(table[...], cross[2 * p + h])) * norm
                for d in (1, 2):
                    live = jnp.full((CH, LAGS), reach, jnp.int32) >= d
                    stage[2 * p + h, d] = jnp.where(live, got[:, (d - 1) * CH : d * CH].T, 0.0)
                write(2 * p + h).start()
        return carry

    lax.fori_loop(0, ROWS // 8, some, 0)

    def written(a, carry):
        write(a).wait()
        return carry

    lax.fori_loop(0, ROWS, written, 0)


def per_device(table, last, spectra, half_width, band):
    norm = 1.0 / math.sqrt(4 * spectra.shape[1] * BINS)
    vmem = pl.BlockSpec(memory_space=pltpu.VMEM)
    smem = pl.BlockSpec(memory_space=pltpu.SMEM)
    sums = pl.pallas_call(
        gather,
        out_shape=[
            pltpu.VMEM((ROWS // 2, LAGS, 2 * CH), f32),
            pltpu.VMEM((ROWS, LAGS, 2 * CH), f32),
            pltpu.VMEM((ROWS, 2 * SPAN, 2 * CH), bf16),
        ],
        in_specs=[pl.BlockSpec(memory_space=pl.ANY), vmem, pl.BlockSpec(memory_space=pl.ANY)],
        out_specs=[vmem, vmem, vmem],
        scratch_shapes=[
            pltpu.VMEM(spectra.shape, bf16),
            pltpu.VMEM(table.shape, bf16),
            pltpu.SemaphoreType.DMA((STEPS + 1,)),
            pltpu.VMEM((3, PIECES, 4, GROUPS, 64, CH), bf16),
            pltpu.VMEM((PIECES, GROUPS, 64, CH), bf16),
            pltpu.VMEM((BINS + SPAN, 4 * CH), bf16),
            pltpu.VMEM((BINS + SPAN, 4 * CH), bf16),
            pltpu.VMEM((8 * SPAN, CH), f32),
            pltpu.VMEM((ROWS, CH), bf16),
            pltpu.VMEM((8, 256), f32),
            pltpu.VMEM((PIECES * GROUPS, 2 * ROWS, 256), f32),
            pltpu.VMEM((ROWS // 2, 2 * SPAN, 2 * CH), bf16),
            pltpu.SemaphoreType.DMA((FLOWS, PIECES)),
            pltpu.SemaphoreType.DMA((FLOWS, PIECES)),
        ],
        compiler_params=pltpu.CompilerParams(collective_id=0, has_side_effects=True, vmem_limit_bytes=VMEM_GATHER),
        cost_estimate=pl.CostEstimate(flops=2 * 5_500_000_000, bytes_accessed=16_000_000, transcendentals=0),
        name="gather",
    )(spectra, half_width.reshape(STEPS, SPAN), table)
    sums = [pltpu.with_memory_space_constraint(x, pltpu.VMEM) for x in sums]
    return pl.pallas_call(
        partial(finish, norm),
        out_shape=jax.ShapeDtypeStruct((ROWS, 3, CH, LAGS), f32),
        in_specs=[smem, vmem, vmem, vmem, vmem],
        out_specs=pl.BlockSpec(memory_space=pl.ANY),
        scratch_shapes=[pltpu.VMEM((ROWS, 3, CH, LAGS), f32), pltpu.SemaphoreType.DMA((ROWS,))],
        compiler_params=pltpu.CompilerParams(vmem_limit_bytes=VMEM_FINISH),
        cost_estimate=pl.CostEstimate(flops=2 * 540_000_000, bytes_accessed=12_600_000, transcendentals=0),
        name="finish",
    )(band, last, *sums)


def solution(mesh):
    table = lag_table()

    def body(spectra, half_width, band):
        return per_device(jnp.asarray(table), jnp.asarray(table[-1]), spectra, half_width, band)

    in_specs = (P(None, "seg", None, "chan"), P(), P())
    out_specs = P(("chan", "seg"), None, None, None)
    return jax.shard_map(body, mesh=mesh, in_specs=in_specs, out_specs=out_specs, check_vma=False)
```

```python
from functools import partial
import math

import jax
import jax.numpy as jnp
import numpy as np
from jax import lax
from jax.experimental import pallas as pl
from jax.experimental.pallas import tpu as pltpu
from jax.sharding import PartitionSpec as P

FLO = 25
NT = 3000
LAGS = 256
BINS = 768
BLOCKS = 32
CH = 128
ROWS = 32
REACH = 16
FLOOR = 0.2

PIECES = 12
WINDOW = 4
LAG_FAR, LAG_ACROSS, LAG_LAST = 2, 4, 5
DOWN = (4,)
GROUPS = BINS // 8 // PIECES
SPAN = 128
STEPS = BINS // SPAN
SHARE = PIECES // STEPS
VMEM_GATHER = 40 * 2**20
VMEM_FINISH = 20 * 2**20

MESH = pl.DeviceIdType.MESH
f32 = jnp.float32
bf16 = jnp.bfloat16

(OWN_SIB, OWN_X, NEAR, LEG1, OWN2_SIB, NEAR2, NEAR_SIB, NEAR2_SIB, LEG2, FAR_SIB, FAR_X, FAR2_SIB) = range(12)
FLOWS = 12
DOWN2, NEAR_X = range(FLOWS, FLOWS + 2)


def lag_table():
    index = np.arange(BINS, dtype=np.int64)
    shifts = np.arange(LAGS, dtype=np.int64) - LAGS // 2 + 1
    phase = ((FLO + index)[:, None] * shifts[None, :]) % NT
    angle = np.float32(2.0 * math.pi / NT) * phase.astype(np.float32)
    angle = angle.astype(np.float64)
    table = np.stack([np.cos(angle), -np.sin(angle)])
    table = table.reshape(2, STEPS, SPAN, LAGS).transpose(1, 3, 0, 2).reshape(STEPS, LAGS, 2 * SPAN)
    return table.astype(np.float32).astype(jnp.bfloat16)


def dot(a, b):
    return lax.dot_general(a, b, (((1,), (0,)), ((), ())), preferred_element_type=f32)


def dot_nt(a, b):
    return lax.dot_general(a, b, (((1,), (1,)), ((), ())), preferred_element_type=f32)


def gather(
    spec_hbm, half, table_hbm, acc0, acc, cross,
    spec, table, load_sem, white, relay, amp_hi, amp_lo, turned, pick, diag, rows32, cross0, ssem, rsem,
):
    def load(m):
        rows = pl.ds(m * SPAN, SPAN)
        return pltpu.make_async_copy(spec_hbm.at[:, :, rows], spec.at[:, :, rows], load_sem.at[m])

    load_table = pltpu.make_async_copy(table_hbm, table, load_sem.at[STEPS])
    for m in range(STEPS):
        load(m).start()
    load_table.start()

    c = lax.axis_index("chan")
    s = lax.axis_index("seg")
    xl = s // 2
    xq = (s + 2) % 4

    def block_at(d):
        t = lax.rem(c + d + 2 * BLOCKS, BLOCKS)
        return t, jnp.where(t // 16 != c // 16, xq, s)

    sib = (c, xl * 2 + 1 - s % 2)
    across = (c, xq)
    near_to = block_at(-1)
    near_from = block_at(1)
    even = c % 2 == 0
    leg_to = block_at(jnp.where(even, 1, -3))
    leg_from = block_at(jnp.where(even, 3, -1))
    nq = near_from[1]
    nq2 = (nq + 2) % 4
    fq = block_at(2)[1]
    fq2 = (fq + 2) % 4
    rq = leg_from[1]

    sends_near, gets_near = c > 0, c < BLOCKS - 1
    sends_far, gets_far = c > 1, c < BLOCKS - 2
    relays = leg_from[0] > 1
    passes_down = sends_near & gets_near

    barrier = pltpu.get_barrier_semaphore()
    greets = ((sib, None), (across, None), (near_to, sends_near), (near_from, gets_near), (leg_to, c != 1), (leg_from, c != BLOCKS - 2))
    greeted = 0
    for d, present in greets:
        greet = partial(pl.semaphore_signal, barrier, inc=1, device_id=d, device_id_type=MESH)
        if present is None:
            greet()
            greeted = greeted + 1
        else:
            pl.when(present)(greet)
            greeted = greeted + present.astype(jnp.int32)

    def copy(flow, j):
        here, there, to, *slot = {
            OWN_SIB: ((0, s), (0, s), sib),
            OWN_X: ((0, s), (0, s), across),
            NEAR: ((0, s), (1, s), near_to),
            LEG1: ((0, s), None, leg_to),
            OWN2_SIB: ((0, xq), (0, xq), sib),
            NEAR2: ((0, xq), (1, xq), near_to),
            NEAR_SIB: ((1, nq), (1, nq), sib),
            NEAR2_SIB: ((1, nq2), (1, nq2), sib),
            LEG2: (None, (2, rq), leg_to),
            FAR_SIB: ((2, fq), (2, fq), sib),
            FAR_X: ((2, fq), (2, fq), across),
            FAR2_SIB: ((2, fq2), (2, fq2), sib),
            DOWN2: ((1, nq), (2, nq), near_to, LEG2),
            NEAR_X: ((1, nq), (1, nq), across, NEAR2),
        }[flow]
        slot = slot[0] if slot else flow
        place = lambda at: relay.at[j] if at is None else white.at[at[0], j, at[1]]
        return pltpu.make_async_remote_copy(
            src_ref=place(here), dst_ref=place(there), send_sem=ssem.at[slot, j], recv_sem=rsem.at[slot, j],
            device_id=to, device_id_type=MESH,
        )

    def start(present, flow, j):
        pl.when(present)(lambda: copy(flow, j).start())

    def plain(j):
        hit = j != DOWN[0]
        for v in DOWN[1:]:
            hit = hit & (j != v)
        return jnp.asarray(hit)

    def down(j):
        return jnp.logical_not(plain(j))

    amp_hi[pl.ds(0, REACH), :] = jnp.zeros((REACH, 4 * CH), bf16)
    amp_lo[pl.ds(0, REACH), :] = jnp.zeros((REACH, 4 * CH), bf16)
    amp_hi[pl.ds(REACH + BINS, SPAN - REACH), :] = jnp.zeros((SPAN - REACH, 4 * CH), bf16)
    amp_lo[pl.ds(REACH + BINS, SPAN - REACH), :] = jnp.zeros((SPAN - REACH, 4 * CH), bf16)

    def amplitude(m, carry):
        load(m).wait()
        rows = pl.ds(pl.multiple_of(m * SPAN, SPAN), SPAN)
        to = pl.ds(pl.multiple_of(m * SPAN + REACH, REACH), SPAN)
        for seg in range(4):
            re = spec[0, seg, rows, :].astype(f32)
            im = spec[1, seg, rows, :].astype(f32)
            a = jnp.sqrt(re * re + im * im)
            hi = a.astype(bf16)
            amp_hi[to, seg * CH : (seg + 1) * CH] = hi
            amp_lo[to, seg * CH : (seg + 1) * CH] = (a - hi.astype(f32)).astype(bf16)
        return carry

    def whiten(m, carry):
        @pl.when(m < STEPS - 1)
        def _():
            amplitude(m + 1, 0)

        rows = pl.ds(pl.multiple_of(m * SPAN, SPAN), SPAN)
        window = pl.ds(pl.multiple_of(m * SPAN, SPAN), 2 * SPAN)
        width = jnp.broadcast_to(half[pl.ds(m, 1), :].astype(f32), (SPAN, SPAN)).T
        width2 = jnp.concatenate([width, width], axis=1)
        row = lax.broadcasted_iota(jnp.int32, (SPAN, 2 * SPAN), 0)
        col = lax.broadcasted_iota(jnp.int32, (SPAN, 2 * SPAN), 1)
        inside = jnp.abs(col - REACH - row).astype(f32) <= width2
        inside = jnp.where(inside, 1.0, 0.0).astype(bf16)
        bin_at = (lax.broadcasted_iota(jnp.int32, (SPAN, SPAN), 0) + m * SPAN).astype(f32)
        count = jnp.minimum(bin_at + width, BINS - 1.0) - jnp.maximum(bin_at - width, 0.0) + 1.0
        total = dot(inside, amp_hi[window, :]) + dot(inside, amp_lo[window, :])
        for seg in range(4):
            denom = jnp.maximum(total[:, seg * CH : (seg + 1) * CH] / count, FLOOR)
            for part in range(2):
                turned[pl.ds((part * 4 + seg) * SPAN, SPAN), :] = spec[part, seg, rows, :].astype(f32) / denom
        for b in range(SPAN // 16):
            block = [turned[pl.ds(b * 16 + t, 8, stride=SPAN), :] for t in range(16)]
            block = jnp.concatenate(block, axis=0).astype(bf16)
            j = m * SHARE + (2 * b) // GROUPS
            white[0, j, s, (2 * b) % GROUPS] = block[:64]
            white[0, j, s, (2 * b + 1) % GROUPS] = block[64:]
        return carry

    def send_own(j):
        copy(OWN_X, j).start()
        start(sends_near, NEAR, j)
        start(sends_far & plain(j), LEG1, j)

    amplitude(0, 0)
    whiten(0, 0)
    pl.semaphore_wait(barrier, greeted)
    for j in range(min(WINDOW, SHARE)):
        send_own(j)
    lax.fori_loop(1, STEPS, whiten, 0)
    for j in range(SHARE, WINDOW):
        send_own(j)

    load_table.wait()

    def clear(d):
        def one(j, carry):
            white[d, j] = jnp.zeros(white.shape[2:], bf16)
            return carry

        lax.fori_loop(0, PIECES, one, 0)

    pl.when(jnp.logical_not(gets_near))(lambda: clear(1))
    pl.when(jnp.logical_not(gets_far))(lambda: clear(2))

    row = lax.broadcasted_iota(jnp.int32, (ROWS, CH), 0)
    col = lax.broadcasted_iota(jnp.int32, (ROWS, CH), 1)
    pick[...] = jnp.where(col == s * ROWS + row, 1.0, 0.0).astype(bf16)
    row = lax.broadcasted_iota(jnp.int32, (8, 256), 0)
    col = lax.broadcasted_iota(jnp.int32, (8, 256), 1)
    diag[...] = jnp.where(row == (col // 8) % 8, 1.0, 0.0)

    def group(d, j, g):
        return white[d, j, :, g].reshape(256, CH)

    def turn_rows(j, g):
        re = dot_nt(pick[...], group(0, j, g))
        col = lax.broadcasted_iota(jnp.int32, (ROWS, 256), 1)
        rows32[j * GROUPS + g, :ROWS] = re
        rows32[j * GROUPS + g, ROWS:] = jnp.where(col % 8 < 4, pltpu.roll(re, 252, 1), -pltpu.roll(re, 4, 1))

    def left(j, g):
        at = j * GROUPS + g
        keep = diag[...]
        parts = [jnp.broadcast_to(rows32[at, pl.ds(r, 1), :], (8, 256)) * keep for r in range(2 * ROWS)]
        return jnp.concatenate(parts, axis=0).astype(bf16)

    def crosses(j, g, slots):
        both = []
        for u in (g, g + 1):
            right = [group(d, j, u) for d in slots]
            right = right[0] if len(right) == 1 else jnp.concatenate(right, axis=1)
            both.append(dot(left(j, u), right).reshape(2 * ROWS, 8, right.shape[1]))
        return jnp.concatenate(both, axis=1).astype(bf16)

    def project(j, count, source, into, first):
        def some(q, carry):
            for u in range(8):
                p = q * 8 + u
                got = dot(table[j // SHARE], source[p])
                into[p] = got if first else into[p] + got
            return carry

        lax.fori_loop(0, count // 8, some, 0)

    def project_at(j, count, source, into, pieces):
        pl.when(j == SHARE - 1)(lambda: project(j, count, source, into, True))
        later = (j % SHARE == SHARE - 1) & (j > SHARE - 1) & (j < pieces)
        pl.when(later)(lambda: project(j, count, source, into, False))

    def bins_at(j, i, part):
        return pl.ds(pl.multiple_of(part * SPAN + (j % SHARE) * (8 * GROUPS) + i * 16, 16), 16)

    def compute0(j):
        copy(OWN_SIB, j).wait_recv()
        copy(OWN2_SIB, j).wait_recv()
        for g in range(GROUPS):
            turn_rows(j, g)
        for i in range(GROUPS // 2):
            got = crosses(j, 2 * i, (0,)).reshape(2, ROWS // 2, 2, 16, CH)
            for part in range(2):
                for h in range(2):
                    cross0[:, bins_at(j, i, part), h * CH : (h + 1) * CH] = got[part, :, h]
        project_at(j, ROWS // 2, cross0, acc0, PIECES)

    def compute12(j):
        @pl.when(gets_near)
        def _():
            copy(NEAR_SIB, j).wait_recv()
            copy(NEAR2_SIB, j).wait_recv()

        @pl.when(gets_far)
        def _():
            copy(FAR_SIB, j).wait_recv()
            copy(FAR2_SIB, j).wait_recv()

        for i in range(GROUPS // 2):
            got = crosses(j, 2 * i, (1, 2)).reshape(2, ROWS, 16, 2 * CH)
            for part in range(2):
                cross[:, bins_at(j, i, part), :] = got[part]
        project_at(j, ROWS, cross, acc, PIECES - SHARE)

    def own_arrived(j):
        copy(OWN_X, j).wait_recv()
        start(sends_near & plain(j), NEAR2, j)
        copy(OWN_SIB, j).start()
        copy(OWN2_SIB, j).start()

        @pl.when(relays & plain(j))
        def _():
            copy(LEG1, j).wait_recv()
            copy(LEG2, j).start()

        @pl.when(gets_near)
        def _():
            copy(NEAR, j).wait_recv()
            start(sends_near & down(j), DOWN2, j)
            start(down(j), NEAR_X, j)
            copy(NEAR_SIB, j).start()

    def far_arrived(j):
        @pl.when(gets_far)
        def _():
            copy(LEG2, j).wait_recv()
            copy(FAR_X, j).start()
            copy(FAR_SIB, j).start()

        @pl.when(gets_near)
        def _():
            copy(NEAR2, j).wait_recv()
            copy(NEAR2_SIB, j).start()

    def far_across(j):
        @pl.when(gets_far)
        def _():
            copy(FAR_X, j).wait_recv()
            copy(FAR2_SIB, j).start()

    def sent(j):
        for flow in (OWN_SIB, OWN_X, OWN2_SIB):
            copy(flow, j).wait_send()
        for flow, present in (
            (NEAR, sends_near), (NEAR_SIB, gets_near), (NEAR2_SIB, gets_near), (FAR_SIB, gets_far), (FAR_X, gets_far),
            (FAR2_SIB, gets_far), (LEG1, sends_far & plain(j)), (LEG2, relays & plain(j)), (NEAR2, sends_near & plain(j)),
            (DOWN2, passes_down & down(j)), (NEAR_X, gets_near & down(j)),
        ):
            pl.when(present)(copy(flow, j).wait_send)

    def step(t, carry):
        pl.when(t + WINDOW < PIECES)(lambda: send_own(t + WINDOW))
        pl.when(t < PIECES)(lambda: own_arrived(t))
        pl.when((t >= 1) & (t < PIECES + 1))(lambda: compute0(t - 1))
        pl.when((t >= LAG_FAR) & (t < PIECES + LAG_FAR))(lambda: far_arrived(t - LAG_FAR))
        pl.when((t >= LAG_ACROSS) & (t < PIECES + LAG_ACROSS))(lambda: far_across(t - LAG_ACROSS))
        pl.when(t >= LAG_LAST)(lambda: compute12(t - LAG_LAST))
        pl.when(t >= LAG_LAST)(lambda: sent(t - LAG_LAST))
        return carry

    lax.fori_loop(0, PIECES + LAG_LAST, step, 0)


def finish(norm, band, table, acc0, acc, cross, out, stage, sem):
    c = lax.axis_index("chan")
    reach = jnp.minimum(band[c], BLOCKS - 1 - c)

    def write(a):
        return pltpu.make_async_copy(stage.at[a], out.at[a], sem.at[a])

    def some(q, carry):
        for p in [4 * q + u for u in range(4)]:
            for h in range(2):
                stage[2 * p + h, 0] = (acc0[p, :, h * CH : (h + 1) * CH] * norm).T
                got = (acc[2 * p + h] + dot(table[...], cross[2 * p + h])) * norm
                for d in (1, 2):
                    live = jnp.full((CH, LAGS), reach, jnp.int32) >= d
                    stage[2 * p + h, d] = jnp.where(live, got[:, (d - 1) * CH : d * CH].T, 0.0)
                write(2 * p + h).start()
        return carry

    lax.fori_loop(0, ROWS // 8, some, 0)

    def written(a, carry):
        write(a).wait()
        return carry

    lax.fori_loop(0, ROWS, written, 0)


def per_device(table, last, spectra, half_width, band):
    norm = 1.0 / math.sqrt(4 * spectra.shape[1] * BINS)
    vmem = pl.BlockSpec(memory_space=pltpu.VMEM)
    smem = pl.BlockSpec(memory_space=pltpu.SMEM)
    sums = pl.pallas_call(
        gather,
        out_shape=[
            pltpu.VMEM((ROWS // 2, LAGS, 2 * CH), f32),
            pltpu.VMEM((ROWS, LAGS, 2 * CH), f32),
            pltpu.VMEM((ROWS, 2 * SPAN, 2 * CH), bf16),
        ],
        in_specs=[pl.BlockSpec(memory_space=pl.ANY), vmem, pl.BlockSpec(memory_space=pl.ANY)],
        out_specs=[vmem, vmem, vmem],
        scratch_shapes=[
            pltpu.VMEM(spectra.shape, bf16),
            pltpu.VMEM(table.shape, bf16),
            pltpu.SemaphoreType.DMA((STEPS + 1,)),
            pltpu.VMEM((3, PIECES, 4, GROUPS, 64, CH), bf16),
            pltpu.VMEM((PIECES, GROUPS, 64, CH), bf16),
            pltpu.VMEM((BINS + SPAN, 4 * CH), bf16),
            pltpu.VMEM((BINS + SPAN, 4 * CH), bf16),
            pltpu.VMEM((8 * SPAN, CH), f32),
            pltpu.VMEM((ROWS, CH), bf16),
            pltpu.VMEM((8, 256), f32),
            pltpu.VMEM((PIECES * GROUPS, 2 * ROWS, 256), f32),
            pltpu.VMEM((ROWS // 2, 2 * SPAN, 2 * CH), bf16),
            pltpu.SemaphoreType.DMA((FLOWS, PIECES)),
            pltpu.SemaphoreType.DMA((FLOWS, PIECES)),
        ],
        compiler_params=pltpu.CompilerParams(collective_id=0, has_side_effects=True, vmem_limit_bytes=VMEM_GATHER),
        cost_estimate=pl.CostEstimate(flops=2 * 5_500_000_000, bytes_accessed=16_000_000, transcendentals=0),
        name="gather",
    )(spectra, half_width.reshape(STEPS, SPAN), table)
    sums = [pltpu.with_memory_space_constraint(x, pltpu.VMEM) for x in sums]
    return pl.pallas_call(
        partial(finish, norm),
        out_shape=jax.ShapeDtypeStruct((ROWS, 3, CH, LAGS), f32),
        in_specs=[smem, vmem, vmem, vmem, vmem],
        out_specs=pl.BlockSpec(memory_space=pl.ANY),
        scratch_shapes=[pltpu.VMEM((ROWS, 3, CH, LAGS), f32), pltpu.SemaphoreType.DMA((ROWS,))],
        compiler_params=pltpu.CompilerParams(vmem_limit_bytes=VMEM_FINISH),
        cost_estimate=pl.CostEstimate(flops=2 * 540_000_000, bytes_accessed=12_600_000, transcendentals=0),
        name="finish",
    )(band, last, *sums)


def solution(mesh):
    table = lag_table()

    def body(spectra, half_width, band):
        return per_device(jnp.asarray(table), jnp.asarray(table[-1]), spectra, half_width, band)

    in_specs = (P(None, "seg", None, "chan"), P(), P())
    out_specs = P(("chan", "seg"), None, None, None)
    return jax.shard_map(body, mesh=mesh, in_specs=in_specs, out_specs=out_specs, check_vma=False)
```
